32 devices in a mesh: ctx: 16 (over z, x, core), head: 2 (over y).
Axes of the slice: x: 2, y: 2, z: 4, core: 2. Of those that a mesh axis runs over, the one named last changes fastest.
Arguments:
- queries: bfloat16 [8192, 4096], P(('ctx', 'head')), may hold values from -8 to 8
- key_matrix: bfloat16 [8192, 1024], P(('ctx', 'head')), may hold values from -8 to 8
- values: bfloat16 [8192, 1024], P(('ctx', 'head')), may hold values from -6 to 6
- output_gradient: bfloat16 [8192, 4096], P(('ctx', 'head')), may hold values from -6 to 6
- doc_lens: int32 [16], replicated, may hold values from 1 to 1024, 8192 in all
Outputs:
- grad_queries: bfloat16 [8192, 4096], P(('ctx', 'head'))
- grad_keys: bfloat16 [8192, 1024], P(('ctx', 'head'))
- grad_values: bfloat16 [8192, 1024], P(('ctx', 'head'))
The draws below stay inside these ranges and needn't reach their ends.
Inputs may be any that keep to these rules, and one draw needn't show every extreme that they name: `doc_lens`: documents fill the batch in order; one of them is exactly 1024 tokens long.
All inputs are finite; a program needn't handle non-finite values.
Results may differ from the reference program's by a relative error of at most 0.011.
Values may be sent and summed in bfloat16 or wider, within the bound.
No kernel may reach another device: no remote copies, remote signals or barrier semaphores. Data moves between devices by JAX's collectives and lax.ppermute only.
A program may use at most 128 MiB of HBM per device.

```python
import math
import jax
import jax.numpy as jnp
import numpy as np
from jax import lax

QUERY_HEADS = 32
KEY_VALUE_HEADS = 8
HEAD_SIZE = 128
TOK_DEV = 512
REACH = 2
PACKED_TOKENS = 8192
MAXDOC = 1024
DOCS = 16
N_CTX = 16


def draw_queries(key, part):
    result_output = jnp.clip(jax.random.normal(jax.random.fold_in(key, 21), (PACKED_TOKENS, QUERY_HEADS * HEAD_SIZE), jnp.float32), -6.0, 6.0)
    return result_output.astype(jnp.bfloat16)


def draw_key_matrix(key, part):
    result_output = jnp.clip(jax.random.normal(jax.random.fold_in(key, 22), (PACKED_TOKENS, KEY_VALUE_HEADS * HEAD_SIZE), jnp.float32), -6.0, 6.0)
    return result_output.astype(jnp.bfloat16)


def block_levels(rng, extent, shards, low, top_value):
    def one(axis_at, parts):
        steps = jax.random.uniform(jax.random.fold_in(jax.random.fold_in(rng, 6), axis_at), (parts,), jnp.float32, low / len(shards), top_value / len(shards))
        return jnp.repeat(jnp.exp(steps), extent[axis_at] // parts).reshape((-1,) + (1,) * (len(extent) - axis_at - 1))

    gain = one(*shards[0])
    for cut in shards[1:]:
        gain = gain * one(*cut)
    return gain


def profile(amount, total, most, slope):
    portions = [(1 << 20) // math.isqrt(grade ** slope) + 1 for grade in range(2, amount + 1)]
    surplus, holding = total - most - (amount - 1), [1] * (amount - 1)
    while surplus > 0:
        candidates = [i for i in range(amount - 1) if holding[i] < most]
        whole, left = sum([portions[i] for i in candidates]), surplus
        for i in candidates:
            more = min(most - holding[i], max(1, left * portions[i] // whole), surplus)
            holding[i] = holding[i] + more
            surplus = surplus - more
    return np.array([most] + holding)


def uneven(stream_key, number_of, total, bound, lean):
    if number_of == 2:
        one = jax.random.randint(stream_key, (), max(1, total - bound), min(bound, total - 1) + 1)
        return jnp.stack([one, total - one])
    sizes = jnp.asarray(profile(number_of, total, bound, lean), jnp.int32)
    pairs = (number_of - 1) // 2
    giver, receiver = sizes[1:1 + 2 * pairs:2], sizes[2:2 + 2 * pairs:2]
    slack = jnp.minimum(giver - 1, bound - receiver)
    moved = jax.random.randint(jax.random.fold_in(stream_key, 1), (pairs,), 0, 1 << 20) % (slack + 1)
    sizes = sizes.at[1:1 + 2 * pairs:2].set(giver - moved).at[2:2 + 2 * pairs:2].set(receiver + moved)
    return sizes[jax.random.permutation(jax.random.fold_in(stream_key, 2), number_of)]


def gaussian(key, dims, spread, bound, split=(), held_as=jnp.bfloat16):
    result = jax.random.normal(key, dims, jnp.float32) * spread
    if len(split) > 0:
        result = block_levels(key, dims, split, -0.22, 0.18) * result
    return jnp.clip(result, min=-bound, max=bound).astype(held_as)


def setup_inputs(seed: int = 0) -> dict:
    streams_of = jax.random.split(jax.random.key(seed), 6)
    queries = draw_queries(jax.random.fold_in(streams_of[5], 71), 0)
    key_matrix = draw_key_matrix(jax.random.fold_in(streams_of[5], 71), 0)
    values = gaussian(streams_of[2], (PACKED_TOKENS, KEY_VALUE_HEADS * HEAD_SIZE), 1.0, 6.0, ((0, 32),))
    output_gradient = gaussian(streams_of[3], (PACKED_TOKENS, QUERY_HEADS * HEAD_SIZE), 1.0, 6.0, ((0, 32),))
    doc_lens = uneven(streams_of[4], DOCS, PACKED_TOKENS, MAXDOC, 2).astype(jnp.int32)
    return {"queries": queries, "key_matrix": key_matrix, "values": values, "output_gradient": output_gradient, "doc_lens": doc_lens}


def reference(queries, key_matrix, values, output_gradient, doc_lens):
    head_groups = QUERY_HEADS // KEY_VALUE_HEADS
    window = (REACH + 1) * TOK_DEV
    margin_width = REACH * TOK_DEV
    score_scale = 1.0 / math.sqrt(HEAD_SIZE)
    doc_ends = jnp.cumsum(doc_lens).astype(jnp.int32)
    positions = jnp.arange(PACKED_TOKENS, dtype=jnp.int32)
    token_doc = lax.optimization_barrier(jnp.sum((doc_ends[None, :] <= positions[:, None]).astype(jnp.int32), axis=1)).astype(jnp.int32)
    padded_doc = jnp.concatenate([jnp.full((margin_width,), -1, jnp.int32), token_doc])
    query_head_rows = queries.reshape(PACKED_TOKENS, KEY_VALUE_HEADS, head_groups * HEAD_SIZE).transpose(1, 0, 2)
    head_gradient = output_gradient.reshape(PACKED_TOKENS, KEY_VALUE_HEADS, head_groups * HEAD_SIZE).transpose(1, 0, 2)
    key_head_rows = jnp.pad(key_matrix.reshape(PACKED_TOKENS, KEY_VALUE_HEADS, HEAD_SIZE).transpose(1, 0, 2), ((0, 0), (margin_width, 0), (0, 0)))
    value_head_rows = jnp.pad(values.reshape(PACKED_TOKENS, KEY_VALUE_HEADS, HEAD_SIZE).transpose(1, 0, 2), ((0, 0), (margin_width, 0), (0, 0)))

    def one_head(operands):
        query_all, key_all, value_all, grad_all = operands

        def one_block(accum, block):
            key_acc, value_acc = accum
            start = (block * TOK_DEV).astype(jnp.int32)
            query_rows = lax.dynamic_slice_in_dim(query_all, start, TOK_DEV, 0).reshape(TOK_DEV * head_groups, HEAD_SIZE)
            grad_rows = lax.dynamic_slice_in_dim(grad_all, start, TOK_DEV, 0).reshape(TOK_DEV * head_groups, HEAD_SIZE)
            key_block = lax.dynamic_slice_in_dim(key_all, start, window, 0)
            value_block = lax.dynamic_slice_in_dim(value_all, start, window, 0)
            query_doc = lax.dynamic_slice_in_dim(token_doc, start, TOK_DEV, 0)
            key_doc = lax.dynamic_slice_in_dim(padded_doc, start, window, 0)
            query_pos = start + jnp.arange(TOK_DEV, dtype=jnp.int32)
            key_pos = start - margin_width + jnp.arange(window, dtype=jnp.int32)
            allowed = (key_doc[None, :] == query_doc[:, None]) & (key_pos[None, :] <= query_pos[:, None])
            scores = jnp.dot(query_rows, key_block.T, preferred_element_type=jnp.float32) * score_scale
            scores = jnp.where(allowed[:, None, :], scores.reshape(TOK_DEV, head_groups, window), -1e+30)
            row_max = lax.optimization_barrier(jnp.max(scores, axis=2))
            row_sum = lax.optimization_barrier(jnp.sum(jnp.where(allowed[:, None, :], jnp.exp(scores - row_max[:, :, None]), 0.0), axis=2))
            log_total = row_max + jnp.log(row_sum)
            probability = jnp.where(allowed[:, None, :], jnp.exp(scores - log_total[:, :, None]), 0.0)
            prob_low = probability.astype(jnp.bfloat16).reshape(TOK_DEV * head_groups, window)
            output = jnp.dot(prob_low, value_block, preferred_element_type=jnp.float32)
            row_delta = lax.optimization_barrier(jnp.sum(grad_rows.astype(jnp.float32) * output, axis=1)).reshape(TOK_DEV, head_groups)
            grad_prob = jnp.dot(grad_rows, value_block.T, preferred_element_type=jnp.float32).reshape(TOK_DEV, head_groups, window)
            grad_score = (probability * (grad_prob - row_delta[:, :, None]) * score_scale).astype(jnp.bfloat16)
            grad_score = grad_score.reshape(TOK_DEV * head_groups, window)
            grad_query = jnp.dot(grad_score, key_block, preferred_element_type=jnp.float32).astype(jnp.bfloat16)
            key_grad = jnp.dot(grad_score.T, query_rows, preferred_element_type=jnp.float32)
            value_grad = jnp.dot(prob_low.T, grad_rows, preferred_element_type=jnp.float32)
            key_acc = lax.dynamic_update_slice_in_dim(key_acc, lax.dynamic_slice_in_dim(key_acc, start, window, 0) + key_grad, start, 0)
            value_acc = lax.dynamic_update_slice_in_dim(value_acc, lax.dynamic_slice_in_dim(value_acc, start, window, 0) + value_grad, start, 0)
            return ((key_acc, value_acc), grad_query.reshape(TOK_DEV, head_groups * HEAD_SIZE))
        zeros = jnp.zeros((margin_width + PACKED_TOKENS, HEAD_SIZE), jnp.float32)
        (key_acc, value_acc), grad_query = lax.scan(one_block, (zeros, zeros), jnp.arange(N_CTX, dtype=jnp.int32))
        return (grad_query.reshape(PACKED_TOKENS, head_groups * HEAD_SIZE), key_acc[margin_width:].astype(jnp.bfloat16), value_acc[margin_width:].astype(jnp.bfloat16))
    query_gradient, key_gradient, value_gradient = lax.map(one_head, (query_head_rows, key_head_rows, value_head_rows, head_gradient))
    return (query_gradient.transpose(1, 0, 2).reshape(PACKED_TOKENS, QUERY_HEADS * HEAD_SIZE), key_gradient.transpose(1, 0, 2).reshape(PACKED_TOKENS, KEY_VALUE_HEADS * HEAD_SIZE), value_gradient.transpose(1, 0, 2).reshape(PACKED_TOKENS, KEY_VALUE_HEADS * HEAD_SIZE))
```

```python
import functools
import math

import jax
import jax.numpy as jnp
from jax import lax
from jax.experimental import pallas as pl
from jax.experimental.pallas import tpu as pltpu
from jax.sharding import PartitionSpec as P

QUERY_HEADS = 32
KEY_VALUE_HEADS = 8
GROUP = QUERY_HEADS // KEY_VALUE_HEADS
HEAD_SIZE = 128
REACH = 2
SCALE = 1.0 / math.sqrt(HEAD_SIZE)
NEGATIVE = -1e30
CHUNKS = 4
NT = (((1,), (1,)), ((), ()))


def attend_kernel(n_blocks, bases_of, lens_ref, q_ref, g_ref, *refs):
    kv_refs = refs[:n_blocks]
    refs = refs[n_blocks + 1 :]
    dq_ref, grad_refs = refs[0], refs[1 : 1 + n_blocks]
    bias, q_rows, g_rows, prob, gprob, stats, dq_acc = refs[1 + n_blocks :]
    tokens = q_ref.shape[0]
    keys = kv_refs[0].shape[1]
    rows = GROUP * tokens
    first, bases = bases_of(tokens, keys)

    def add_doc(k, carry):
        end, start = carry
        end = end + lens_ref[k]
        return end, jnp.where(end <= first, end, start)

    _, first_start = lax.fori_loop(0, lens_ref.shape[0], add_doc, (jnp.int32(0), jnp.int32(0)))
    active = [None if b == 0 else (base >= 0) & (first_start < base + keys) for b, base in enumerate(bases)]

    def when_active(b, work):
        if b == 0:
            work()
        else:
            pl.when(active[b])(work)

    @pl.when(pl.program_id(0) == 0)
    def _():
        position = first + lax.broadcasted_iota(jnp.int32, (1, tokens), 1)

        def add_lane_doc(k, carry):
            end, start = carry
            end = end + lens_ref[k]
            return end, jnp.where(end <= position, end, start)

        _, start = lax.fori_loop(
            0, lens_ref.shape[0], add_lane_doc, (jnp.int32(0), jnp.zeros((1, tokens), jnp.int32))
        )
        for b, base in enumerate(bases):

            def fill(b=b, base=base):
                key = base + lax.broadcasted_iota(jnp.int32, (keys, tokens), 0)
                allowed = (key >= start) & (key <= position)
                one = jnp.where(allowed, 0.0, NEGATIVE).astype(jnp.float32)
                bias[b] = jnp.concatenate([one] * GROUP, axis=1)

            when_active(b, fill)

    for j in range(GROUP):
        q_rows[j * tokens : (j + 1) * tokens, :] = q_ref[:, j * HEAD_SIZE : (j + 1) * HEAD_SIZE]
        g_rows[j * tokens : (j + 1) * tokens, :] = g_ref[:, j * HEAD_SIZE : (j + 1) * HEAD_SIZE]

    for b in range(n_blocks):

        def score(b=b):
            s = lax.dot_general(kv_refs[b][0], q_rows[...], NT, preferred_element_type=jnp.float32)
            s = s * (SCALE * math.log2(math.e)) + bias[b]
            top = jnp.max(s, axis=0, keepdims=True)
            p = jnp.exp2(s - top)
            dp = lax.dot_general(kv_refs[b][1], g_rows[...], NT, preferred_element_type=jnp.float32)
            prob[b] = p
            gprob[b] = dp
            stats[b, 0:1] = top
            stats[b, 1:2] = jnp.sum(p, axis=0, keepdims=True)
            stats[b, 2:3] = jnp.sum(p * dp, axis=0, keepdims=True)

        if b > 0:

            @pl.when(jnp.logical_not(active[b]))
            def _(b=b):
                stats[b, 0:1] = jnp.full((1, rows), NEGATIVE, jnp.float32)
                stats[b, 1:3] = jnp.zeros((2, rows), jnp.float32)

        when_active(b, score)

    top = stats[0, 0:1]
    for b in range(1, n_blocks):
        top = jnp.maximum(top, stats[b, 0:1])
    total = jnp.zeros((1, rows), jnp.float32)
    delta = jnp.zeros((1, rows), jnp.float32)
    weights = []
    for b in range(n_blocks):
        w = jnp.exp2(stats[b, 0:1] - top)
        weights.append(w)
        total = total + w * stats[b, 1:2]
        delta = delta + w * stats[b, 2:3]
    inverse = 1.0 / total
    delta = delta * inverse
    for b in range(n_blocks):

        def backward(b=b):
            p = prob[b] * (weights[b] * inverse)
            ds = (p * (gprob[b] - delta)).astype(jnp.bfloat16)
            dv = jnp.dot(p.astype(jnp.bfloat16), g_rows[...], preferred_element_type=jnp.float32)
            dk = jnp.dot(ds, q_rows[...], preferred_element_type=jnp.float32) * SCALE
            grad_refs[b][0] = dk.astype(grad_refs[b].dtype)
            grad_refs[b][1] = dv.astype(grad_refs[b].dtype)
            dq = jnp.dot(kv_refs[b][0].T, ds, preferred_element_type=jnp.float32)
            if b == 0:
                dq_acc[...] = dq
            else:
                dq_acc[...] += dq

        if b > 0:

            @pl.when(jnp.logical_not(active[b]))
            def _(b=b):
                grad_refs[b][...] = jnp.zeros_like(grad_refs[b])

        when_active(b, backward)
    for j in range(GROUP):
        one = dq_acc[:, j * tokens : (j + 1) * tokens].T * SCALE
        dq_ref[:, j * HEAD_SIZE : (j + 1) * HEAD_SIZE] = one.astype(dq_ref.dtype)


def attend(doc_lens, queries, gradients, blocks, bases_of, grad_queries, first_head):
    tokens = queries.shape[0]
    n_blocks = len(blocks)
    keys, width = blocks[0].shape[1:]
    heads = width // HEAD_SIZE
    rows = GROUP * tokens
    wide = pl.BlockSpec((tokens, GROUP * HEAD_SIZE), lambda h: (0, first_head + h))
    pair = pl.BlockSpec((2, keys, HEAD_SIZE), lambda h: (0, 0, h))
    given = [] if grad_queries is None else [grad_queries]
    kernel = functools.partial(attend_kernel, n_blocks, bases_of)
    if grad_queries is None:
        body = lambda *refs: kernel(*refs[: 3 + n_blocks], None, *refs[3 + n_blocks :])
    else:
        body = kernel
    work = heads * rows * keys * n_blocks
    out = pl.pallas_call(
        body,
        grid=(heads,),
        in_specs=[pl.BlockSpec(memory_space=pltpu.SMEM), wide, wide]
        + [pair] * n_blocks
        + [pl.BlockSpec(memory_space=pl.ANY)] * len(given),
        out_specs=[wide] + [pair] * n_blocks,
        out_shape=[jax.ShapeDtypeStruct(queries.shape, jnp.bfloat16)]
        + [jax.ShapeDtypeStruct(x.shape, jnp.bfloat16) for x in blocks],
        scratch_shapes=[
            pltpu.VMEM((n_blocks, keys, rows), jnp.float32),
            pltpu.VMEM((rows, HEAD_SIZE), jnp.bfloat16),
            pltpu.VMEM((rows, HEAD_SIZE), jnp.bfloat16),
            pltpu.VMEM((n_blocks, keys, rows), jnp.float32),
            pltpu.VMEM((n_blocks, keys, rows), jnp.float32),
            pltpu.VMEM((n_blocks, 8, rows), jnp.float32),
            pltpu.VMEM((HEAD_SIZE, rows), jnp.float32),
        ],
        input_output_aliases={3 + n_blocks: 0} if given else {},
        compiler_params=pltpu.CompilerParams(
            dimension_semantics=("arbitrary",), vmem_limit_bytes=48 * 1024 * 1024
        ),
        cost_estimate=pl.CostEstimate(
            flops=10 * work * HEAD_SIZE, bytes_accessed=heads * tokens * 512 * 6, transcendentals=work
        ),
    )(doc_lens, queries, gradients, *blocks, *given)
    return out[0], out[1:]


def flat_route(n_ctx, n_head, step, keep=lambda c, y: True):
    route = []
    for c in range(n_ctx):
        for y in range(n_head):
            to_c, to_y = step(c, y)
            if 0 <= to_c < n_ctx and keep(c, y):
                route.append((c * n_head + y, to_c * n_head + to_y))
    return route


def send(x, route, back=False):
    return lax.ppermute(x, ("ctx", "head"), [(b, a) for a, b in route] if back else route)


def as_f32(*arrays):
    return sum(a.astype(jnp.float32) for a in arrays)


def two_heads(n_ctx, queries, key_matrix, values, gradients, doc_lens):
    fwd = flat_route(n_ctx, 2, lambda c, y: (c + 2, y))
    own_swap = flat_route(n_ctx, 2, lambda c, y: (c, 1 - y), lambda c, y: not (c % 2 == 1 and y == 1))
    far_swap = flat_route(
        n_ctx, 2, lambda c, y: (c, 1 - y), lambda c, y: c >= 2 and not (c % 2 == 0 and y == 0)
    )
    cores = flat_route(n_ctx, 2, lambda c, y: (c + 1 - 2 * (c % 2), y))
    core = lax.axis_index("ctx") % 2
    head = lax.axis_index("head")
    width = key_matrix.shape[1] // CHUNKS

    def bases_of(tokens, keys):
        y = lax.axis_index("head")
        first = (2 * lax.axis_index("ctx") + y) * tokens
        back = [0, 4, 2, 1 + 2 * y, 3 - 2 * y]
        return first, [first - d * tokens for d in back]

    own_parts = []
    windows = []
    for n in range(CHUNKS):
        cut = slice(n * width, (n + 1) * width)
        own = jnp.stack([key_matrix[:, cut], values[:, cut]])
        far = send(own, fwd)
        own_other = send(own, own_swap)
        far_other = send(far, far_swap)
        near1 = send(jnp.where(core == 0, own, far), cores)
        near2 = send(jnp.where(core == 0, own_other, far_other), cores)
        beside = jnp.where(head == 0, far_other, own_other)
        windows.append([own, far, near1, near2, beside])
    grad_queries = None
    key_grads, value_grads = [], []
    for n in range(CHUNKS):
        grad_queries, grads = attend(
            doc_lens, queries, gradients, windows[n], bases_of, grad_queries, n * (width // HEAD_SIZE)
        )
        g_own, g_far, g_near1, g_near2, g_beside = grads
        back1 = send(g_near1, cores)
        back2 = send(g_near2, cores)
        zero = jnp.zeros((), jnp.float32)
        own_other = as_f32(jnp.where(core == 0, back2, 0)) + jnp.where(head == 1, as_f32(g_beside), zero)
        far_other = as_f32(jnp.where(core == 1, back2, 0)) + jnp.where(head == 0, as_f32(g_beside), zero)
        far_sum = send(far_other.astype(jnp.bfloat16), far_swap, back=True)
        own_sum = send(own_other.astype(jnp.bfloat16), own_swap, back=True)
        far_all = as_f32(g_far, far_sum) + jnp.where(core == 1, as_f32(back1), zero)
        arrived = send(far_all.astype(jnp.bfloat16), fwd, back=True)
        mine = as_f32(g_own, own_sum, arrived) + jnp.where(core == 0, as_f32(back1), zero)
        mine = mine.astype(jnp.bfloat16)
        key_grads.append(mine[0])
        value_grads.append(mine[1])
    return grad_queries, jnp.concatenate(key_grads, axis=1), jnp.concatenate(value_grads, axis=1)


def any_heads(n_ctx, queries, key_matrix, values, gradients, doc_lens):
    kv = lax.all_gather(jnp.stack([key_matrix, values]), "head", axis=1, tiled=True)
    block = kv.shape[1]
    routes = [[(c, c + d) for c in range(n_ctx - d)] for d in range(1, REACH + 1)]
    window = [kv] + [lax.ppermute(kv, "ctx", route) for route in routes]

    def bases_of(tokens, keys):
        base = lax.axis_index("ctx") * keys
        return base + lax.axis_index("head") * tokens, [base - d * keys for d in range(REACH + 1)]

    grad_queries, grads = attend(doc_lens, queries, gradients, window, bases_of, None, 0)
    total = grads[0].astype(jnp.float32)
    for grad, route in zip(grads[1:], routes):
        total = total + lax.ppermute(grad, "ctx", [(b, a) for a, b in route]).astype(jnp.float32)
    mine = lax.psum_scatter(total, "head", scatter_dimension=1, tiled=True).astype(jnp.bfloat16)
    return grad_queries, mine[0], mine[1]


def solution(mesh):
    rows = P(("ctx", "head"), None)
    n_ctx, n_head = mesh.shape["ctx"], mesh.shape["head"]
    plan = two_heads if n_head == 2 else any_heads
    return jax.shard_map(
        functools.partial(plan, n_ctx),
        mesh=mesh,
        in_specs=(rows, rows, rows, rows, P()),
        out_specs=(rows, rows, rows),
        check_vma=False,
    )
```

```python
import collections
import functools
import math

import jax
import jax.numpy as jnp
from jax import lax
from jax.experimental import pallas as pl
from jax.experimental.pallas import tpu as pltpu
from jax.sharding import PartitionSpec as P

QUERY_HEADS = 32
KEY_VALUE_HEADS = 8
GROUP = QUERY_HEADS // KEY_VALUE_HEADS
HEAD_SIZE = 128
REACH = 2
SCALE = 1.0 / math.sqrt(HEAD_SIZE)
NEGATIVE = -1e30
CHUNKS = ((4,), (4,))
COST = 4
NT = (((1,), (1,)), ((), ()))

Plan = collections.namedtuple("Plan", ["inputs", "blocks", "grad_leads", "place", "pick", "give"])


def attend_kernel(plan, lens_ref, q_ref, g_ref, *refs):
    n_in, n_out = plan.inputs, len(plan.grad_leads)
    in_refs, refs = refs[:n_in], refs[n_in:]
    dq_ref, grad_outs, mark = refs[0], refs[1 : 1 + n_out], refs[1 + n_out]
    window, grads, bias, q_rows, g_rows, prob, gprob, dq_acc = refs[2 + n_out :]
    mark[0] = 0
    tokens = q_ref.shape[0]
    n_blocks, _, keys, _ = window.shape
    rows = GROUP * tokens
    first, own_base = plan.place(tokens, keys)

    def add_doc(k, carry):
        end, start = carry
        end = end + lens_ref[k]
        return end, jnp.where(end <= first, end, start)

    _, first_start = lax.fori_loop(0, lens_ref.shape[0], add_doc, (jnp.int32(0), jnp.int32(0)))
    n_active = 1 + lax.div(jnp.maximum(own_base - first_start, 0) + keys - 1, keys)

    @pl.when(pl.program_id(0) == 0)
    def _():
        position = first + lax.broadcasted_iota(jnp.int32, (1, tokens), 1)

        def add_lane_doc(k, carry):
            end, start = carry
            end = end + lens_ref[k]
            return end, jnp.where(end <= position, end, start)

        _, start = lax.fori_loop(
            0, lens_ref.shape[0], add_lane_doc, (jnp.int32(0), jnp.zeros((1, tokens), jnp.int32))
        )

        @pl.loop(0, n_active)
        def _(b):
            key = own_base - b * keys + lax.broadcasted_iota(jnp.int32, (keys, tokens), 0)
            allowed = (key >= start) & (key <= position)
            one = jnp.where(allowed, 0.0, NEGATIVE).astype(jnp.float32)
            bias[b] = jnp.concatenate([one] * GROUP, axis=1).reshape(keys // 8, 8, rows)

    plan.pick(in_refs, window)
    for j in range(GROUP):
        q_rows[j * tokens : (j + 1) * tokens, :] = q_ref[:, j * HEAD_SIZE : (j + 1) * HEAD_SIZE]
        g_rows[j * tokens : (j + 1) * tokens, :] = g_ref[:, j * HEAD_SIZE : (j + 1) * HEAD_SIZE]

    def some_blocks(n):
        top = None
        for b in range(n):
            s = lax.dot_general(window[b, 0], q_rows[...], NT, preferred_element_type=jnp.float32)
            s = s.reshape(keys // 8, 8, rows) * (SCALE * math.log2(math.e)) + bias[b]
            prob[b] = s
            best = jnp.max(s, axis=0)
            top = best if b == 0 else jnp.maximum(top, best)
        top = jnp.broadcast_to(jnp.max(top, axis=0, keepdims=True), (8, rows))
        total = jnp.zeros((8, rows), jnp.float32)
        delta = jnp.zeros((8, rows), jnp.float32)
        for b in range(n):
            dp = lax.dot_general(window[b, 1], g_rows[...], NT, preferred_element_type=jnp.float32)
            dp = dp.reshape(keys // 8, 8, rows)
            p = jnp.exp2(prob[b] - top[None])
            prob[b] = p
            gprob[b] = dp
            total = total + jnp.sum(p, axis=0)
            delta = delta + jnp.sum(p * dp, axis=0)
        inverse = 1.0 / jnp.sum(total, axis=0, keepdims=True)
        delta = jnp.broadcast_to(jnp.sum(delta, axis=0, keepdims=True) * inverse, (8, rows))
        inverse = jnp.broadcast_to(inverse, (8, rows))
        dq = None
        for b in range(n):
            p = prob[b] * inverse[None]
            ds = (p * (gprob[b] - delta[None])).reshape(keys, rows).astype(jnp.bfloat16)
            p = p.reshape(keys, rows).astype(jnp.bfloat16)
            dv = jnp.dot(p, g_rows[...], preferred_element_type=jnp.float32)
            dk = jnp.dot(ds, q_rows[...], preferred_element_type=jnp.float32) * SCALE
            grads[b, 0] = dk.astype(grads.dtype)
            grads[b, 1] = dv.astype(grads.dtype)
            one = jnp.dot(window[b, 0].T, ds, preferred_element_type=jnp.float32)
            dq = one if b == 0 else dq + one
        dq_acc[...] = dq

    for n in range(1, n_blocks + 1):
        pl.when(n_active == n)(functools.partial(some_blocks, n))

    @pl.loop(n_active, n_blocks)
    def _(b):
        grads[b] = jnp.zeros(grads.shape[1:], grads.dtype)

    plan.give(grads, grad_outs)
    for j in range(GROUP):
        one = dq_acc[:, j * tokens : (j + 1) * tokens].T * SCALE
        dq_ref[:, j * HEAD_SIZE : (j + 1) * HEAD_SIZE] = one.astype(dq_ref.dtype)


def attend(doc_lens, queries, gradients, arrays, plan, head, start, heads, grad_queries=None):
    tokens = queries.shape[0]
    keys = arrays[0].shape[1]
    width = heads * HEAD_SIZE
    rows = GROUP * tokens
    n_blocks = plan.blocks
    wide = pl.BlockSpec((tokens, GROUP * HEAD_SIZE), lambda h: (0, head + h))

    def pairs(leads, at):
        return [pl.BlockSpec((lead, keys, HEAD_SIZE), lambda h: (0, 0, at + h)) for lead in leads]

    given = [] if grad_queries is None else [grad_queries]
    n_given = 3 + len(arrays)

    def body(*refs):
        attend_kernel(plan, *refs[:n_given], *refs[n_given + len(given) :])

    work = heads * rows * keys * n_blocks
    out = pl.pallas_call(
        body,
        grid=(heads,),
        in_specs=[pl.BlockSpec(memory_space=pltpu.SMEM), wide, wide]
        + pairs([x.shape[0] for x in arrays], start)
        + [pl.BlockSpec(memory_space=pl.ANY)] * len(given),
        out_specs=[wide] + pairs(plan.grad_leads, 0) + [pl.BlockSpec(memory_space=pltpu.SMEM)],
        out_shape=[jax.ShapeDtypeStruct(queries.shape, jnp.bfloat16)]
        + [jax.ShapeDtypeStruct((lead, keys, width), jnp.bfloat16) for lead in plan.grad_leads]
        + [jax.ShapeDtypeStruct((1,), jnp.int32)],
        scratch_shapes=[
            pltpu.VMEM((n_blocks, 2, keys, HEAD_SIZE), jnp.bfloat16),
            pltpu.VMEM((n_blocks, 2, keys, HEAD_SIZE), jnp.bfloat16),
            pltpu.VMEM((n_blocks, keys // 8, 8, rows), jnp.float32),
            pltpu.VMEM((rows, HEAD_SIZE), jnp.bfloat16),
            pltpu.VMEM((rows, HEAD_SIZE), jnp.bfloat16),
            pltpu.VMEM((n_blocks, keys // 8, 8, rows), jnp.float32),
            pltpu.VMEM((n_blocks, keys // 8, 8, rows), jnp.float32),
            pltpu.VMEM((HEAD_SIZE, rows), jnp.float32),
        ],
        input_output_aliases={n_given: 0} if given else {},
        compiler_params=pltpu.CompilerParams(
            dimension_semantics=("arbitrary",), vmem_limit_bytes=58 * 1024 * 1024
        ),
        cost_estimate=pl.CostEstimate(
            flops=COST * 10 * work * HEAD_SIZE, bytes_accessed=heads * tokens * 512 * 6, transcendentals=work
        ),
    )(doc_lens, queries, gradients, *arrays, *given)
    return out[0], out[1:-1], out[-1][0]


def flat_route(n_ctx, n_head, step, keep=lambda c, y: True):
    route = []
    for c in range(n_ctx):
        for y in range(n_head):
            to_c, to_y = step(c, y)
            if 0 <= to_c < n_ctx and keep(c, y):
                route.append((c * n_head + y, to_c * n_head + to_y))
    return route


def send(x, route, back=False):
    return lax.ppermute(x, ("ctx", "head"), [(b, a) for a, b in route] if back else route)


def gate(x, *after):
    return lax.optimization_barrier((x, *after))[0]


def as_f32(*arrays):
    return sum(a.astype(jnp.float32) for a in arrays)


def two_heads(n_ctx, queries, key_matrix, values, gradients, doc_lens):
    fwd = flat_route(n_ctx, 2, lambda c, y: (c + 2, y))
    own_swap = flat_route(n_ctx, 2, lambda c, y: (c, 1 - y), lambda c, y: not (c % 2 == 1 and y == 1))
    far_swap = flat_route(
        n_ctx, 2, lambda c, y: (c, 1 - y), lambda c, y: c >= 2 and not (c % 2 == 0 and y == 0)
    )
    cores = flat_route(n_ctx, 2, lambda c, y: (c + 1 - 2 * (c % 2), y))
    core = lax.axis_index("ctx") % 2
    head_index = lax.axis_index("head")

    def place(tokens, keys):
        first = (2 * lax.axis_index("ctx") + lax.axis_index("head")) * tokens
        return first, first

    def pick(refs, window):
        own, far, near, own_other, far_other = refs
        even = lax.axis_index("head") == 0
        window[0] = own[...]
        window[1] = jnp.where(even, near[2:4], own_other[...])
        window[2] = near[0:2]
        window[3] = jnp.where(even, far_other[...], near[2:4])
        window[4] = far[...]

    def give(grads, outs):
        own, far, near, beside = outs
        even = lax.axis_index("head") == 0
        own[...] = grads[0]
        far[...] = grads[4]
        near[0:2] = grads[2]
        near[2:4] = jnp.where(even, grads[1], grads[3])
        beside[...] = jnp.where(even, grads[3], grads[1])

    plan = Plan(5, 5, [2, 2, 4, 2], place, pick, give)

    def choose(zero, own, far, own_other, far_other):
        return jnp.where(core + zero == 0, jnp.concatenate([own, own_other]), jnp.concatenate([far, far_other]))

    arrived, head = [], 0
    for sizes in CHUNKS:
        cut = slice(head * HEAD_SIZE, (head + sum(sizes)) * HEAD_SIZE)
        own = jnp.stack([key_matrix[:, cut], values[:, cut]])
        if arrived:
            own = gate(own, arrived[-1][1])
        far, own_other = send(own, fwd), send(own, own_swap)
        if not arrived:
            far = gate(far, own_other)
        arrived.append((own, far, own_other, send(far, far_swap)))
        head += sum(sizes)
    zero = jnp.zeros((), jnp.float32)

    def to_pair(grads, after):
        near, beside = grads[2:]
        back = send(gate(near, *after), cores)
        back1, back2 = back[:2], back[2:]
        own_grad = as_f32(jnp.where(core == 0, back2, 0)) + jnp.where(head_index == 1, as_f32(beside), zero)
        far_grad = as_f32(jnp.where(core == 1, back2, 0)) + jnp.where(head_index == 0, as_f32(beside), zero)
        return back1, own_grad.astype(jnp.bfloat16), far_grad.astype(jnp.bfloat16)

    def to_far(far, far_sum, back1, mark):
        total = as_f32(far, far_sum) + jnp.where(core + mark == 1, as_f32(back1), zero)
        return total.astype(jnp.bfloat16)

    grad_queries, mark, head = None, 0, 0
    swapped, chip = None, None
    key_grads, value_grads = [], []

    def finish(own, back1, own_sum, arriving):
        total = as_f32(own, own_sum, arriving) + jnp.where(core == 0, as_f32(back1), zero)
        total = total.astype(jnp.bfloat16)
        key_grads.append(total[0])
        value_grads.append(total[1])

    for n, sizes in enumerate(CHUNKS):
        own, far, own_other, far_other = arrived[n]
        coming = list(arrived[n + 1]) if n + 1 < len(CHUNKS) else []
        if n == 0:
            near = choose(mark, own, gate(far, *coming[1:2]), own_other, far_other)
        else:
            near = choose(mark, own, far, own_other, far_other)
        near = send(near, cores)
        start = 0
        for i, heads in enumerate(sizes):
            window = [own, far, near, own_other, far_other]
            if swapped:
                window[2] = gate(near, *swapped[2])
            grad_queries, grads, mark = attend(
                doc_lens, queries, gradients, window, plan, head, start, heads, grad_queries
            )
            start, head = start + heads, head + heads
            after = coming[2:] if i + 1 == len(sizes) else []
            if chip:
                after = after + [chip[3]]
                finish(*chip)
                chip = None
            if swapped:
                (g_own, g_far), (back1, far_sum, own_sum), _ = swapped
                far_all = to_far(g_far, far_sum, back1, mark)
                after = after + [far_all, own_sum]
                chip = (g_own, back1, own_sum, send(far_all, fwd, back=True))
            back1, own_grad, far_grad = to_pair(grads, after)
            far_sum = send(far_grad, far_swap, back=True)
            own_sum = send(own_grad, own_swap, back=True)
            swapped = (grads[:2], (back1, far_sum, own_sum), (own_grad, far_grad))
    if chip:
        finish(*chip)
    (g_own, g_far), (back1, far_sum, own_sum), _ = swapped
    finish(g_own, back1, own_sum, send(to_far(g_far, far_sum, back1, 0), fwd, back=True))
    return grad_queries, jnp.concatenate(key_grads, axis=1), jnp.concatenate(value_grads, axis=1)


def any_heads(n_ctx, queries, key_matrix, values, gradients, doc_lens):
    kv = lax.all_gather(jnp.stack([key_matrix, values]), "head", axis=1, tiled=True)
    block = kv.shape[1]
    routes = [[(c, c + d) for c in range(n_ctx - d)] for d in range(1, REACH + 1)]
    window = [kv] + [lax.ppermute(kv, "ctx", route) for route in routes]

    def place(tokens, keys):
        base = lax.axis_index("ctx") * keys
        return base + lax.axis_index("head") * tokens, base

    def pick(refs, window):
        for b, ref in enumerate(refs):
            window[b] = ref[...]

    def give(grads, outs):
        for b, ref in enumerate(outs):
            ref[...] = grads[b]

    plan = Plan(REACH + 1, REACH + 1, [2] * (REACH + 1), place, pick, give)
    grad_queries, grads, _ = attend(doc_lens, queries, gradients, window, plan, 0, 0, KEY_VALUE_HEADS)
    total = grads[0].astype(jnp.float32)
    for grad, route in zip(grads[1:], routes):
        total = total + lax.ppermute(grad, "ctx", [(b, a) for a, b in route]).astype(jnp.float32)
    mine = lax.psum_scatter(total, "head", scatter_dimension=1, tiled=True).astype(jnp.bfloat16)
    return grad_queries, mine[0], mine[1]


def solution(mesh):
    rows = P(("ctx", "head"), None)
    n_ctx, n_head = mesh.shape["ctx"], mesh.shape["head"]
    plan = two_heads if n_head == 2 else any_heads
    return jax.shard_map(
        functools.partial(plan, n_ctx),
        mesh=mesh,
        in_specs=(rows, rows, rows, rows, P()),
        out_specs=(rows, rows, rows),
        check_vma=False,
    )
```

```python
import collections
import functools
import math

import jax
import jax.numpy as jnp
from jax import lax
from jax.experimental import pallas as pl
from jax.experimental.pallas import tpu as pltpu
from jax.sharding import PartitionSpec as P

QUERY_HEADS = 32
KEY_VALUE_HEADS = 8
GROUP = QUERY_HEADS // KEY_VALUE_HEADS
HEAD_SIZE = 128
REACH = 2
SCALE = 1.0 / math.sqrt(HEAD_SIZE)
NEGATIVE = -1e30
CHUNKS = ((4,), (4,))
COST = 4
NT = (((1,), (1,)), ((), ()))

Plan = collections.namedtuple("Plan", ["inputs", "blocks", "grad_leads", "place", "pick", "give"])


def attend_kernel(plan, lens_ref, q_ref, g_ref, *refs):
    n_in, n_out = plan.inputs, len(plan.grad_leads)
    in_refs, refs = refs[:n_in], refs[n_in:]
    dq_ref, grad_outs, mark = refs[0], refs[1 : 1 + n_out], refs[1 + n_out]
    window, grads, bias, q_rows, g_rows, prob, gprob, dq_acc = refs[2 + n_out :]
    mark[0] = 0
    tokens = q_ref.shape[0]
    n_blocks, _, keys, _ = window.shape
    rows = GROUP * tokens
    first, own_base = plan.place(tokens, keys)

    def add_doc(k, carry):
        end, start = carry
        end = end + lens_ref[k]
        return end, jnp.where(end <= first, end, start)

    _, first_start = lax.fori_loop(0, lens_ref.shape[0], add_doc, (jnp.int32(0), jnp.int32(0)))
    n_active = 1 + lax.div(jnp.maximum(own_base - first_start, 0) + keys - 1, keys)

    @pl.when(pl.program_id(0) == 0)
    def _():
        position = first + lax.broadcasted_iota(jnp.int32, (1, tokens), 1)

        def add_lane_doc(k, carry):
            end, start = carry
            end = end + lens_ref[k]
            return end, jnp.where(end <= position, end, start)

        _, start = lax.fori_loop(
            0, lens_ref.shape[0], add_lane_doc, (jnp.int32(0), jnp.zeros((1, tokens), jnp.int32))
        )

        @pl.loop(0, n_active)
        def _(b):
            key = own_base - b * keys + lax.broadcasted_iota(jnp.int32, (keys, tokens), 0)
            allowed = (key >= start) & (key <= position)
            one = jnp.where(allowed, 0.0, NEGATIVE).astype(jnp.float32)
            bias[b] = jnp.concatenate([one] * GROUP, axis=1).reshape(keys // 8, 8, rows)

    plan.pick(in_refs, window)
    for j in range(GROUP):
        q_rows[j * tokens : (j + 1) * tokens, :] = q_ref[:, j * HEAD_SIZE : (j + 1) * HEAD_SIZE]
        g_rows[j * tokens : (j + 1) * tokens, :] = g_ref[:, j * HEAD_SIZE : (j + 1) * HEAD_SIZE]

    def some_blocks(n):
        top = None
        for b in range(n):
            s = lax.dot_general(window[b, 0], q_rows[...], NT, preferred_element_type=jnp.float32)
            s = s.reshape(keys // 8, 8, rows) * (SCALE * math.log2(math.e)) + bias[b]
            prob[b] = s
            best = jnp.max(s, axis=0)
            top = best if b == 0 else jnp.maximum(top, best)
        top = jnp.broadcast_to(jnp.max(top, axis=0, keepdims=True), (8, rows))
        total = jnp.zeros((8, rows), jnp.float32)
        delta = jnp.zeros((8, rows), jnp.float32)
        for b in range(n):
            dp = lax.dot_general(window[b, 1], g_rows[...], NT, preferred_element_type=jnp.float32)
            dp = dp.reshape(keys // 8, 8, rows)
            p = jnp.exp2(prob[b] - top[None])
            prob[b] = p
            gprob[b] = dp
            total = total + jnp.sum(p, axis=0)
            delta = delta + jnp.sum(p * dp, axis=0)
        inverse = 1.0 / jnp.sum(total, axis=0, keepdims=True)
        delta = jnp.broadcast_to(jnp.sum(delta, axis=0, keepdims=True) * inverse, (8, rows))
        inverse = jnp.broadcast_to(inverse, (8, rows))
        dq = None
        for b in range(n):
            p = prob[b] * inverse[None]
            ds = (p * (gprob[b] - delta[None])).reshape(keys, rows).astype(jnp.bfloat16)
            p = p.reshape(keys, rows).astype(jnp.bfloat16)
            dv = jnp.dot(p, g_rows[...], preferred_element_type=jnp.float32)
            dk = jnp.dot(ds, q_rows[...], preferred_element_type=jnp.float32) * SCALE
            grads[b, 0] = dk.astype(grads.dtype)
            grads[b, 1] = dv.astype(grads.dtype)
            one = jnp.dot(window[b, 0].T, ds, preferred_element_type=jnp.float32)
            dq = one if b == 0 else dq + one
        dq_acc[...] = dq

    for n in range(1, n_blocks + 1):
        pl.when(n_active == n)(functools.partial(some_blocks, n))

    @pl.loop(n_active, n_blocks)
    def _(b):
        grads[b] = jnp.zeros(grads.shape[1:], grads.dtype)

    plan.give(grads, grad_outs)
    for j in range(GROUP):
        one = dq_acc[:, j * tokens : (j + 1) * tokens].T * SCALE
        dq_ref[:, j * HEAD_SIZE : (j + 1) * HEAD_SIZE] = one.astype(dq_ref.dtype)


def attend(doc_lens, queries, gradients, arrays, plan, head, start, heads, grad_queries=None):
    tokens = queries.shape[0]
    keys = arrays[0].shape[1]
    width = heads * HEAD_SIZE
    rows = GROUP * tokens
    n_blocks = plan.blocks
    wide = pl.BlockSpec((tokens, GROUP * HEAD_SIZE), lambda h: (0, head + h))

    def pairs(leads, at):
        return [pl.BlockSpec((lead, keys, HEAD_SIZE), lambda h: (0, 0, at + h)) for lead in leads]

    given = [] if grad_queries is None else [grad_queries]
    n_given = 3 + len(arrays)

    def body(*refs):
        attend_kernel(plan, *refs[:n_given], *refs[n_given + len(given) :])

    work = heads * rows * keys * n_blocks
    out = pl.pallas_call(
        body,
        grid=(heads,),
        in_specs=[pl.BlockSpec(memory_space=pltpu.SMEM), wide, wide]
        + pairs([x.shape[0] for x in arrays], start)
        + [pl.BlockSpec(memory_space=pl.ANY)] * len(given),
        out_specs=[wide] + pairs(plan.grad_leads, 0) + [pl.BlockSpec(memory_space=pltpu.SMEM)],
        out_shape=[jax.ShapeDtypeStruct(queries.shape, jnp.bfloat16)]
        + [jax.ShapeDtypeStruct((lead, keys, width), jnp.bfloat16) for lead in plan.grad_leads]
        + [jax.ShapeDtypeStruct((1,), jnp.int32)],
        scratch_shapes=[
            pltpu.VMEM((n_blocks, 2, keys, HEAD_SIZE), jnp.bfloat16),
            pltpu.VMEM((n_blocks, 2, keys, HEAD_SIZE), jnp.bfloat16),
            pltpu.VMEM((n_blocks, keys // 8, 8, rows), jnp.float32),
            pltpu.VMEM((rows, HEAD_SIZE), jnp.bfloat16),
            pltpu.VMEM((rows, HEAD_SIZE), jnp.bfloat16),
            pltpu.VMEM((n_blocks, keys // 8, 8, rows), jnp.float32),
            pltpu.VMEM((n_blocks, keys // 8, 8, rows), jnp.float32),
            pltpu.VMEM((HEAD_SIZE, rows), jnp.float32),
        ],
        input_output_aliases={n_given: 0} if given else {},
        compiler_params=pltpu.CompilerParams(
            dimension_semantics=("arbitrary",), vmem_limit_bytes=58 * 1024 * 1024
        ),
        cost_estimate=pl.CostEstimate(
            flops=COST * 10 * work * HEAD_SIZE, bytes_accessed=heads * tokens * 512 * 6, transcendentals=work
        ),
    )(doc_lens, queries, gradients, *arrays, *given)
    return out[0], out[1:-1], out[-1][0]


def flat_route(n_ctx, n_head, step, keep=lambda c, y: True):
    route = []
    for c in range(n_ctx):
        for y in range(n_head):
            to_c, to_y = step(c, y)
            if 0 <= to_c < n_ctx and keep(c, y):
                route.append((c * n_head + y, to_c * n_head + to_y))
    return route


def send(x, route, back=False):
    return lax.ppermute(x, ("ctx", "head"), [(b, a) for a, b in route] if back else route)


def gate(x, *after):
    return lax.optimization_barrier((x, *after))[0]


def as_f32(*arrays):
    return sum(a.astype(jnp.float32) for a in arrays)


def two_heads(n_ctx, queries, key_matrix, values, gradients, doc_lens):
    fwd = flat_route(n_ctx, 2, lambda c, y: (c + 2, y))
    own_swap = flat_route(n_ctx, 2, lambda c, y: (c, 1 - y), lambda c, y: not (c % 2 == 1 and y == 1))
    far_swap = flat_route(
        n_ctx, 2, lambda c, y: (c, 1 - y), lambda c, y: c >= 2 and not (c % 2 == 0 and y == 0)
    )
    far_part = [(a, b) for a, b in far_swap if a // 2 % 2 == 1]
    side = flat_route(n_ctx, 2, lambda c, y: (c + 2, y), lambda c, y: c % 2 == 0 and y == 0)
    cores = flat_route(n_ctx, 2, lambda c, y: (c + 1 - 2 * (c % 2), y))
    core = lax.axis_index("ctx") % 2
    head_index = lax.axis_index("head")

    def place(tokens, keys):
        first = (2 * lax.axis_index("ctx") + lax.axis_index("head")) * tokens
        return first, first

    def pick(refs, window):
        own, far, near, own_other, far_other = refs
        even = lax.axis_index("head") == 0
        window[0] = own[...]
        window[1] = jnp.where(even, near[2:4], own_other[...])
        window[2] = near[0:2]
        window[3] = jnp.where(even, far_other[...], near[2:4])
        window[4] = far[...]

    def give(grads, outs):
        own, far, near, beside = outs
        even = lax.axis_index("head") == 0
        own[...] = grads[0]
        far[...] = grads[4]
        near[0:2] = grads[2]
        near[2:4] = jnp.where(even, grads[1], grads[3])
        beside[...] = jnp.where(even, grads[3], grads[1])

    plan = Plan(5, 5, [2, 2, 4, 2], place, pick, give)

    def choose(zero, own, far, own_other, far_other):
        return jnp.where(core + zero == 0, jnp.concatenate([own, own_other]), jnp.concatenate([far, far_other]))

    arrived, head = [], 0
    for sizes in CHUNKS:
        cut = slice(head * HEAD_SIZE, (head + sum(sizes)) * HEAD_SIZE)
        own = jnp.stack([key_matrix[:, cut], values[:, cut]])
        if arrived:
            own = gate(own, arrived[-1][1])
        far, own_other = send(own, fwd), send(own, own_swap)
        if not arrived:
            far = gate(far, own_other)
        far_other = send(far, far_swap)
        arrived.append((own, far, own_other, far_other))
        head += sum(sizes)
    zero = jnp.zeros((), jnp.float32)

    def to_pair(grads, after, final):
        near, beside = grads[2:]
        back = send(gate(near, *after), cores)
        back1, back2 = back[:2], back[2:]
        far_grad = as_f32(jnp.where(core == 1, back2, 0)) + jnp.where(head_index == 0, as_f32(beside), zero)
        far_grad = far_grad.astype(jnp.bfloat16)
        own_grad = as_f32(jnp.where(core == 0, back2, 0)) + jnp.where(head_index == 1, as_f32(beside), zero)
        if final:
            own_grad = own_grad + as_f32(send(far_grad, side, back=True))
        return back1, own_grad.astype(jnp.bfloat16), far_grad

    def to_far(far, far_sum, back1, mark):
        total = as_f32(far, far_sum) + jnp.where(core + mark == 1, as_f32(back1), zero)
        return total.astype(jnp.bfloat16)

    grad_queries, mark, head = None, 0, 0
    swapped, chip = None, None
    key_grads, value_grads = [], []

    def finish(own, back1, own_sum, arriving):
        for i, parts in enumerate((key_grads, value_grads)):
            total = as_f32(own[i], own_sum[i], arriving[i]) + jnp.where(core == 0, as_f32(back1[i]), zero)
            parts.append(total.astype(jnp.bfloat16))

    for n, sizes in enumerate(CHUNKS):
        own, far, own_other, far_other = arrived[n]
        coming = list(arrived[n + 1]) if n + 1 < len(CHUNKS) else []
        if n == 0:
            near = choose(mark, own, gate(far, *coming[1:2]), own_other, far_other)
        else:
            near = choose(mark, own, far, own_other, far_other)
        near = send(near, cores)
        start = 0
        for i, heads in enumerate(sizes):
            window = [own, far, near, own_other, far_other]
            if swapped:
                window[2] = gate(near, *swapped[2])
            grad_queries, grads, mark = attend(
                doc_lens, queries, gradients, window, plan, head, start, heads, grad_queries
            )
            start, head = start + heads, head + heads
            after = coming[2:] if i + 1 == len(sizes) else []
            if chip:
                after = after + [chip[3]]
                finish(*chip)
                chip = None
            if swapped:
                (g_own, g_far), (back1, far_sum, own_sum), _ = swapped
                far_all = to_far(g_far, far_sum, back1, mark)
                after = after + [far_all, own_sum]
                chip = (g_own, back1, own_sum, send(far_all, fwd, back=True))
            final = head == sum(map(sum, CHUNKS))
            back1, own_grad, far_grad = to_pair(grads, after, final)
            far_sum = send(far_grad, far_part if final else far_swap, back=True)
            own_sum = send(own_grad, own_swap, back=True)
            swapped = (grads[:2], (back1, far_sum, own_sum), (own_grad, far_grad))
    if chip:
        finish(*chip)
    (g_own, g_far), (back1, far_sum, own_sum), _ = swapped
    finish(g_own, back1, own_sum, send(to_far(g_far, far_sum, back1, 0), fwd, back=True))
    return grad_queries, jnp.concatenate(key_grads, axis=1), jnp.concatenate(value_grads, axis=1)


def any_heads(n_ctx, queries, key_matrix, values, gradients, doc_lens):
    kv = lax.all_gather(jnp.stack([key_matrix, values]), "head", axis=1, tiled=True)
    block = kv.shape[1]
    routes = [[(c, c + d) for c in range(n_ctx - d)] for d in range(1, REACH + 1)]
    window = [kv] + [lax.ppermute(kv, "ctx", route) for route in routes]

    def place(tokens, keys):
        base = lax.axis_index("ctx") * keys
        return base + lax.axis_index("head") * tokens, base

    def pick(refs, window):
        for b, ref in enumerate(refs):
            window[b] = ref[...]

    def give(grads, outs):
        for b, ref in enumerate(outs):
            ref[...] = grads[b]

    plan = Plan(REACH + 1, REACH + 1, [2] * (REACH + 1), place, pick, give)
    grad_queries, grads, _ = attend(doc_lens, queries, gradients, window, plan, 0, 0, KEY_VALUE_HEADS)
    total = grads[0].astype(jnp.float32)
    for grad, route in zip(grads[1:], routes):
        total = total + lax.ppermute(grad, "ctx", [(b, a) for a, b in route]).astype(jnp.float32)
    mine = lax.psum_scatter(total, "head", scatter_dimension=1, tiled=True).astype(jnp.bfloat16)
    return grad_queries, mine[0], mine[1]


def solution(mesh):
    rows = P(("ctx", "head"), None)
    n_ctx, n_head = mesh.shape["ctx"], mesh.shape["head"]
    plan = two_heads if n_head == 2 else any_heads
    return jax.shard_map(
        functools.partial(plan, n_ctx),
        mesh=mesh,
        in_specs=(rows, rows, rows, rows, P()),
        out_specs=(rows, rows, rows),
        check_vma=False,
    )
```
